32 devices in a mesh: pitch: 4 (over z), radial: 4 (over y, core), axial: 2 (over x).
Axes of the slice: x: 2, y: 2, z: 4, core: 2. Of those that a mesh axis runs over, the one named last changes fastest.
Arguments:
- density: float32 [9, 4, 32, 512], P(None, 'axial', 'radial', 'pitch'), may hold values from 0.5 to 2
- moments: float32 [9, 4, 4, 32, 512], P(None, None, 'axial', 'radial', 'pitch'), may hold values from -6 to 6
- shifts: int32 [9], replicated, may hold values from 0 to 511, as said below
Outputs:
- residual: float32 [9, 5, 4, 32, 512], P(None, None, 'axial', 'radial', 'pitch')
- update: float32 [9, 5, 4, 32, 512], P(None, None, 'axial', 'radial', 'pitch')
The draws below stay inside these ranges and needn't reach their ends.
Inputs may be any that keep to these rules, and one draw needn't show every extreme that they name: `shifts`: every instance's offset lies in 0 to 511 and some instance has offset 512 - 1.
All inputs are finite; a program needn't handle non-finite values.
Results may differ from the reference program's by a relative error of at most 0.0005.
Values sent between devices are 32-bit elements; how exact they have to be, the bound alone decides.
A program may use at most 192 MiB of HBM per device.

```python
import math
import jax
import jax.numpy as jnp
import numpy as np
from jax import lax

INST = 9
A_DEV = 2
NPITCH = 512
NRAD = 32
NAX = 4


def draw_shifts(key, part):
    drawn = jax.random.randint(jax.random.fold_in(key, 11), (INST,), 0, NPITCH)
    picked = jax.random.randint(jax.random.fold_in(key, 12), (), 0, INST)
    return jnp.where(jnp.arange(INST) == picked, NPITCH - 1, drawn).astype(jnp.int32)


def shard_levels(stream_key, shape, shards, least, largest):
    level = 1.0
    for dim, blocks in shards:
        draws = jax.random.uniform(jax.random.fold_in(jax.random.fold_in(stream_key, 6), dim), (blocks,), jnp.float32, least / len(shards), largest / len(shards))
        level = level * jnp.repeat(jnp.exp(draws), shape[dim] // blocks).reshape((-1,) + (1,) * (len(shape) - 1 - dim))
    return level


def centred(stream_key, shape, scale, most, split=(), kind=jnp.bfloat16):
    gain = shard_levels(stream_key, shape, split, -0.22, 0.18) if split else 1.0
    values = jax.random.normal(stream_key, shape, jnp.float32) * scale * gain
    return jnp.minimum(jnp.maximum(values, -most), most).astype(kind)


def setup_inputs(seed: int = 0) -> dict:
    arg_keys = jax.random.split(jax.random.key(seed), 4)
    return {
        "density": jnp.clip(jnp.exp(math.log(2.0) - 1.3862944 * jax.random.uniform(arg_keys[0], (INST, NAX, NRAD, NPITCH), jnp.float32) ** shard_levels(arg_keys[0], (INST, NAX, NRAD, NPITCH), ((1, 2), (2, 4), (3, 4)), -0.2, 0.2)), 0.5, 2.0),
        "moments": centred(arg_keys[1], (INST, 4, NAX, NRAD, NPITCH), 1.0, 6.0, ((2, 2), (3, 4), (4, 4)), jnp.float32),
        "shifts": draw_shifts(jax.random.fold_in(arg_keys[3], 71), 0),
    }


COEFFS = (0.75, -0.15, 1.0 / 60.0)
GAMMA_LESS = 0.4


def spectral_table(count):
    points = np.arange(count)
    spread = points[:, None] - points[None, :]
    nonzero = np.where(spread == 0, 1, spread)
    entries = 0.5 * np.where(spread % 2 == 0, 1.0, -1.0) / np.sin(np.pi * nonzero / count)
    return jnp.asarray(np.where(spread == 0, 0.0, entries), jnp.float32)


def fluxes(density, moments):
    axial_m = moments[:, 0]
    radial_m = moments[:, 1]
    pitch_m = moments[:, 2]
    energy = moments[:, 3]
    pressure = GAMMA_LESS * (energy - 0.5 * (axial_m * axial_m + radial_m * radial_m + pitch_m * pitch_m) / density)
    pitch_v = pitch_m / density
    radial_v = radial_m / density
    along_pitch = jnp.stack([pitch_m, axial_m * pitch_v, radial_m * pitch_v, pitch_m * pitch_v + pressure, (energy + pressure) * pitch_v], axis=1)
    along_radial = jnp.stack([radial_m, axial_m * radial_v, radial_m * radial_v + pressure, pitch_m * radial_v, (energy + pressure) * radial_v], axis=1)
    return along_pitch, along_radial


def reference(density, moments, shifts):
    fields = jnp.concatenate([density[:, None], moments], axis=1)
    along_pitch, along_radial = fluxes(density, moments)
    deriv_p = jnp.zeros_like(fields)
    for offset, weight in enumerate(COEFFS):
        reach = offset + 1
        deriv_p = deriv_p + weight * (jnp.roll(along_pitch, -reach, axis=4) - jnp.roll(along_pitch, reach, axis=4))
    padded = jnp.pad(along_radial, ((0, 0), (0, 0), (0, 0), (3, 3), (0, 0)))
    deriv_r = jnp.zeros_like(fields)
    for offset, weight in enumerate(COEFFS):
        reach = offset + 1
        deriv_r = deriv_r + weight * (padded[:, :, :, 3 + reach:3 + reach + NRAD] - padded[:, :, :, 3 - reach:3 - reach + NRAD])
    spectral = jnp.einsum("nm,mvarp->nvarp", spectral_table(INST), fields, precision=lax.Precision.HIGHEST)
    rotor = fields[:, :, A_DEV - 1]
    stator = fields[:, :, A_DEV]
    columns = jnp.arange(NPITCH, dtype=jnp.int32)
    to_stator_idx = (columns[None, :] - shifts[:, None]) % NPITCH
    to_rotor_idx = (columns[None, :] + shifts[:, None]) % NPITCH
    to_stator = jnp.take_along_axis(rotor, to_stator_idx[:, None, None, :], axis=3)
    to_rotor = jnp.take_along_axis(stator, to_rotor_idx[:, None, None, :], axis=3)
    residual = deriv_p + deriv_r + spectral
    residual = residual.at[:, :, A_DEV - 1].add(to_rotor - rotor)
    residual = residual.at[:, :, A_DEV].add(to_stator - stator)
    smooth_eps = float(NPITCH * NPITCH // 16)
    modes = jnp.arange(NPITCH).astype(jnp.float32)
    eigen = 1.0 + 2.0 * smooth_eps - 2.0 * smooth_eps * jnp.cos(2.0 * np.pi * modes / NPITCH)
    update = jnp.real(jnp.fft.ifft(jnp.fft.fft(residual, axis=-1) / eigen, axis=-1)).astype(jnp.float32)
    return residual, update
```

```python
import functools
import math

import jax
import jax.numpy as jnp
import numpy as np
from jax import lax
from jax.experimental import pallas as pl
from jax.experimental.pallas import tpu as pltpu
from jax.sharding import PartitionSpec as P

COEFFS = (0.75, -0.15, 1.0 / 60.0)
GAMMA_LESS = 0.4
HIGHEST = lax.Precision.HIGHEST
MESH = pl.DeviceIdType.MESH
VMEM = pl.BlockSpec(memory_space=pltpu.VMEM)
SMEM = pl.BlockSpec(memory_space=pltpu.SMEM)
CHUNKS = 3


def filter_constants(extent):
    eps = float(extent * extent // 16)
    decay = 2.0 * eps / (1.0 + 2.0 * eps + math.sqrt(1.0 + 4.0 * eps))
    gain = 1.0 / (math.sqrt(1.0 + 4.0 * eps) * (1.0 - decay**extent))
    return decay, gain


def tables(width, extent):
    decay, gain = filter_constants(extent)
    points = np.arange(width)
    apart = np.abs(points[:, None] - points[None, :])
    green = gain * (decay**apart + decay ** (extent - apart))
    deriv = np.zeros((width, width))
    rims = np.zeros((8, width))
    picks = np.zeros((8, width))
    for offset, weight in enumerate(COEFFS):
        reach = offset + 1
        for i in range(width):
            if i + reach < width:
                deriv[i + reach, i] += weight
            else:
                rims[i + reach - width, i] += weight
            if i - reach >= 0:
                deriv[i - reach, i] -= weight
            else:
                rims[4 + i - reach + 3, i] -= weight
    for h in range(3):
        picks[h, h] = 1.0
        picks[4 + h, width - 3 + h] = 1.0
    sums = np.zeros((8, width))
    sums[0] = decay ** (width - 1.0 - points)
    sums[1] = decay ** (points + 0.0)
    spread = np.zeros((8, width))
    spread[0] = gain * decay ** (points + 1.0)
    spread[1] = gain * decay ** (width - points + 0.0)
    return np.concatenate([deriv, green, rims, picks, sums, spread]).astype(np.float32)


def dot(a, b):
    return jnp.dot(a, b, precision=HIGHEST, preferred_element_type=jnp.float32)


def dot_nt(a, b):
    return lax.dot_general(
        a, b, (((1,), (1,)), ((), ())), precision=HIGHEST, preferred_element_type=jnp.float32
    )


def dot_tn(a, b):
    return lax.dot_general(
        a, b, (((0,), (0,)), ((), ())), precision=HIGHEST, preferred_element_type=jnp.float32
    )


def exchange_kernel(
    count_p,
    count_r,
    density,
    moments,
    table,
    base,
    smoothed,
    whole,
    along_p,
    along_r,
    rim_out,
    rim_in,
    sum_out,
    sum_in,
    cross_send,
    cross_recv,
    chain_send,
    chain_recv,
    rim_send,
    rim_recv,
    radial_send,
    radial_recv,
    sum_send,
    sum_recv,
):
    inst, planes, rad, width = density.shape
    rows = inst * 5 * planes * rad
    extent = width * count_p
    decay, _ = filter_constants(extent)
    p = lax.axis_index("pitch")
    r = lax.axis_index("radial")
    a = lax.axis_index("axial")
    plane = (planes - 1) * (1 - a)
    per = inst // CHUNKS

    barrier = pltpu.get_barrier_semaphore()
    for k in range(1, count_p):
        pl.semaphore_signal(
            barrier, inc=1, device_id=(lax.rem(p + k, count_p), r, a), device_id_type=MESH
        )
    for k in (1, count_r - 1):
        pl.semaphore_signal(
            barrier, inc=1, device_id=(p, lax.rem(r + k, count_r), a), device_id_type=MESH
        )
    pl.semaphore_signal(barrier, inc=1, device_id=(p, r, 1 - a), device_id_type=MESH)

    rho = density[...]
    axial_m, radial_m, pitch_m, energy = (moments[:, v] for v in range(4))
    inverse = 1.0 / rho
    pressure = GAMMA_LESS * (
        energy - 0.5 * (axial_m * axial_m + radial_m * radial_m + pitch_m * pitch_m) * inverse
    )
    pitch_v = pitch_m * inverse
    radial_v = radial_m * inverse
    enthalpy = energy + pressure
    along_p[:, 0] = pitch_m
    along_p[:, 1] = axial_m * pitch_v
    along_p[:, 2] = radial_m * pitch_v
    along_p[:, 3] = pitch_m * pitch_v + pressure
    along_p[:, 4] = enthalpy * pitch_v
    mine = slice(rad, 2 * rad)
    along_r[:, 0, :, mine] = radial_m
    along_r[:, 1, :, mine] = axial_m * radial_v
    along_r[:, 2, :, mine] = radial_m * radial_v + pressure
    along_r[:, 3, :, mine] = pitch_m * radial_v
    along_r[:, 4, :, mine] = enthalpy * radial_v

    @pl.when(r == 0)
    def _():
        along_r[:, :, :, 0:rad] = jnp.zeros((inst, 5, planes, rad, width), jnp.float32)

    @pl.when(r == count_r - 1)
    def _():
        along_r[:, :, :, 2 * rad : 3 * rad] = jnp.zeros(
            (inst, 5, planes, rad, width), jnp.float32
        )

    pl.semaphore_wait(barrier, count_p + 2)

    def cross(c, part):
        span = pl.ds(c * per, per)
        if part == 0:
            src, dst = density.at[span, plane], whole.at[p, span, 0]
        else:
            src, dst = moments.at[span, :, plane], whole.at[p, span, 1:5]
        return pltpu.make_async_remote_copy(
            src_ref=src,
            dst_ref=dst,
            send_sem=cross_send.at[c, part],
            recv_sem=cross_recv.at[c, part],
            device_id=(p, r, 1 - a),
            device_id_type=MESH,
        )

    for c in range(CHUNKS):
        for part in range(2):
            cross(c, part).start()

    def radial_copy(up):
        if up:
            src = along_r.at[:, :, :, 2 * rad - 3 : 2 * rad]
            dst = along_r.at[:, :, :, rad - 3 : rad]
            target = r + 1
        else:
            src = along_r.at[:, :, :, rad : rad + 3]
            dst = along_r.at[:, :, :, 2 * rad : 2 * rad + 3]
            target = r - 1
        return pltpu.make_async_remote_copy(
            src_ref=src,
            dst_ref=dst,
            send_sem=radial_send.at[int(up)],
            recv_sem=radial_recv.at[int(up)],
            device_id=(p, target, a),
            device_id_type=MESH,
        )

    @pl.when(r < count_r - 1)
    def _():
        radial_copy(True).start()

    @pl.when(r > 0)
    def _():
        radial_copy(False).start()

    flat_p = along_p[...].reshape(rows, width)
    rim_out[...] = dot_nt(table[2 * width + 8 : 2 * width + 16], flat_p)

    def rim_copy(up):
        part = slice(4, 8) if up else slice(0, 4)
        return pltpu.make_async_remote_copy(
            src_ref=rim_out.at[part],
            dst_ref=rim_in.at[part],
            send_sem=rim_send.at[int(up)],
            recv_sem=rim_recv.at[int(up)],
            device_id=(lax.rem(p + (1 if up else count_p - 1), count_p), r, a),
            device_id_type=MESH,
        )

    rim_copy(True).start()
    rim_copy(False).start()

    def chain(s, c, up):
        block = p - (s - 1) if up else p + (s - 1)
        span = pl.ds(c * per, per)
        part = whole.at[block, span]
        return pltpu.make_async_remote_copy(
            src_ref=part,
            dst_ref=part,
            send_sem=chain_send.at[int(up), s - 1, c],
            recv_sem=chain_recv.at[int(up), s - 1, c],
            device_id=(p + 1 if up else p - 1, r, a),
            device_id_type=MESH,
        )

    def arrival(s, c, up):
        block = p - s if up else p + s
        span = pl.ds(c * per, per)
        part = whole.at[block, span]
        return pltpu.make_async_remote_copy(
            src_ref=part,
            dst_ref=part,
            send_sem=chain_send.at[int(up), s - 1, c],
            recv_sem=chain_recv.at[int(up), s - 1, c],
            device_id=(p - 1 if up else p + 1, r, a),
            device_id_type=MESH,
        )

    def sends(s, up):
        if up:
            return jnp.logical_and(p < count_p - 1, p - (s - 1) >= 0)
        return jnp.logical_and(p > 0, p + (s - 1) < count_p)

    def receives(s, up):
        return p - s >= 0 if up else p + s < count_p

    def first_step(c):
        cross(c, 0).wait_recv()
        cross(c, 1).wait_recv()
        for up in (True, False):
            pl.when(sends(1, up))(lambda up=up: chain(1, c, up).start())

    def later_step(s, c):
        for up in (True, False):
            pl.when(receives(s - 1, up))(lambda up=up: arrival(s - 1, c, up).wait_recv())
            pl.when(sends(s, up))(lambda up=up: chain(s, c, up).start())

    fields = [rho] + [axial_m, radial_m, pitch_m, energy]
    partial = dot(flat_p, table[0:width])
    base[...] = partial.reshape(inst, 5, planes, rad, width)
    for v, field in enumerate(fields):
        total = None
        for k in range(1, (inst + 1) // 2):
            weight = 0.5 * (-1.0) ** k / math.sin(math.pi * k / inst)
            back = jnp.concatenate([field[inst - k :], field[: inst - k]], axis=0)
            ahead = jnp.concatenate([field[k:], field[:k]], axis=0)
            term = weight * (back - ahead)
            total = term if total is None else total + term
        for b in range(planes):
            on = jnp.where(plane == b, 1.0, 0.0).astype(jnp.float32)
            base[:, v, b] += total[:, b] - on * field[:, b]

    first_step(0)

    pl.when(r > 0)(lambda: radial_copy(True).wait_recv())
    pl.when(r < count_r - 1)(lambda: radial_copy(False).wait_recv())
    rim_copy(True).wait_recv()
    rim_copy(False).wait_recv()
    across = dot_tn(rim_in[...], table[2 * width : 2 * width + 8])
    radial = None
    for offset, weight in enumerate(COEFFS):
        k = offset + 1
        term = weight * (
            along_r[:, :, :, rad + k : 2 * rad + k] - along_r[:, :, :, rad - k : 2 * rad - k]
        )
        radial = term if radial is None else radial + term
    base[...] += across.reshape(inst, 5, planes, rad, width) + radial
    flat = base[...].reshape(rows, width)
    sum_out[...] = dot_nt(table[2 * width + 16 : 2 * width + 24], flat)

    def sum_copy(k):
        return pltpu.make_async_remote_copy(
            src_ref=sum_out.at[0:2],
            dst_ref=sum_in.at[k - 1],
            send_sem=sum_send.at[k - 1],
            recv_sem=sum_recv.at[k - 1],
            device_id=(lax.rem(p + k, count_p), r, a),
            device_id_type=MESH,
        )

    for k in range(1, count_p):
        sum_copy(k).start()
    for c in range(1, CHUNKS):
        first_step(c)
    smoothed[...] = dot(flat, table[width : 2 * width]).reshape(inst, 5, planes, rad, width)
    for c in range(CHUNKS):
        later_step(2, c)
    ahead = None
    behind = None
    for k in range(1, count_p):
        sum_copy(k).wait_recv()
        left = decay ** (width * (k - 1.0)) * sum_in[k - 1, 0:1]
        right = decay ** (width * (count_p - k - 1.0)) * sum_in[k - 1, 1:2]
        ahead = left if ahead is None else ahead + left
        behind = right if behind is None else behind + right
    carried = jnp.concatenate([ahead, behind, jnp.zeros((6, rows), jnp.float32)], axis=0)
    smoothed[...] += dot_tn(carried, table[2 * width + 24 : 2 * width + 32]).reshape(
        inst, 5, planes, rad, width
    )
    for s in range(3, count_p):
        for c in range(CHUNKS):
            later_step(s, c)

    for c in range(CHUNKS):
        for up in (True, False):
            last = count_p - 1
            pl.when(receives(last, up))(
                lambda c=c, up=up: arrival(last, c, up).wait_recv()
            )
            for s in range(1, count_p):
                pl.when(sends(s, up))(lambda s=s, c=c, up=up: chain(s, c, up).wait_send())
        cross(c, 0).wait_send()
        cross(c, 1).wait_send()
    pl.when(r < count_r - 1)(lambda: radial_copy(True).wait_send())
    pl.when(r > 0)(lambda: radial_copy(False).wait_send())
    rim_copy(True).wait_send()
    rim_copy(False).wait_send()
    for k in range(1, count_p):
        sum_copy(k).wait_send()


def finish_kernel(
    count_p, shifts, table, whole, base, smoothed, residual, update, aligned, before, after
):
    inst, _, planes, rad, width = base.shape
    extent = width * count_p
    decay, _ = filter_constants(extent)
    log_decay = math.log(decay)
    p = lax.axis_index("pitch")
    a = lax.axis_index("axial")
    plane = (planes - 1) * (1 - a)
    lane = lax.broadcasted_iota(jnp.int32, (rad, width), 1)
    group = 5 * rad
    for n in range(inst):
        offset = jnp.where(a == 1, shifts[n], extent - shifts[n])
        start = lax.rem(p * width - offset + 2 * extent, extent)
        block = lax.div(start, width)
        inside = start - block * width
        near = whole[block, n]
        far = whole[lax.rem(block + 1, count_p), n]
        merged = jnp.where((lane >= inside)[None], near, far).reshape(group, width)
        aligned[n * group : (n + 1) * group] = pltpu.roll(
            merged, lax.rem(width - inside, width), 1
        )
        left = None
        right = None
        for b in range(count_p):
            spacing = start - 1 - b * width - lane
            spacing = jnp.where(spacing < 0, spacing + extent, spacing)
            outside = spacing < extent - width
            gap = spacing.astype(jnp.float32)
            up = jnp.where(outside, jnp.exp(gap * log_decay), 0.0)
            down = jnp.where(outside, jnp.exp((extent - width - 1.0 - gap) * log_decay), 0.0)
            block_b = whole[b, n]
            left = block_b * up[None] if left is None else left + block_b * up[None]
            right = block_b * down[None] if right is None else right + block_b * down[None]
        before[n * group : (n + 1) * group] = left.reshape(group, width)
        after[n * group : (n + 1) * group] = right.reshape(group, width)
    spread = table[2 * width + 24 : 2 * width + 32]
    ahead = jnp.sum(before[...], axis=1, keepdims=True)
    behind = jnp.sum(after[...], axis=1, keepdims=True)
    filtered = dot(aligned[...], table[width : 2 * width])
    filtered = filtered + ahead * spread[0:1] + behind * spread[1:2]
    shape = (inst, 5, rad, width)
    residual[...] = base[...]
    update[...] = smoothed[...]
    residual[:, :, plane] += aligned[...].reshape(shape)
    update[:, :, plane] += filtered.reshape(shape)


def local(density, moments, shifts):
    count_p = lax.axis_size("pitch")
    count_r = lax.axis_size("radial")
    inst, planes, rad, width = density.shape
    rows = inst * 5 * planes * rad
    table = jnp.asarray(tables(width, width * count_p))
    block = jax.ShapeDtypeStruct((inst, 5, planes, rad, width), jnp.float32)
    dma = pltpu.SemaphoreType.DMA
    base, smoothed, whole = pl.pallas_call(
        functools.partial(exchange_kernel, count_p, count_r),
        out_shape=(
            block,
            block,
            jax.ShapeDtypeStruct((count_p, inst, 5, rad, width), jnp.float32),
        ),
        in_specs=[VMEM] * 3,
        out_specs=(VMEM,) * 3,
        scratch_shapes=[
            pltpu.VMEM((inst, 5, planes, rad, width), jnp.float32),
            pltpu.VMEM((inst, 5, planes, 3 * rad, width), jnp.float32),
            pltpu.VMEM((8, rows), jnp.float32),
            pltpu.VMEM((8, rows), jnp.float32),
            pltpu.VMEM((8, rows), jnp.float32),
            pltpu.VMEM((count_p - 1, 2, rows), jnp.float32),
            dma((CHUNKS, 2)),
            dma((CHUNKS, 2)),
            dma((2, count_p - 1, CHUNKS)),
            dma((2, count_p - 1, CHUNKS)),
            dma((2,)),
            dma((2,)),
            dma((2,)),
            dma((2,)),
            dma((count_p - 1,)),
            dma((count_p - 1,)),
        ],
        compiler_params=pltpu.CompilerParams(
            collective_id=0, has_side_effects=True, vmem_limit_bytes=40 * 2**20
        ),
        name="exchange",
    )(density, moments, table)
    return pl.pallas_call(
        functools.partial(finish_kernel, count_p),
        out_shape=(block, block),
        in_specs=[SMEM] + [VMEM] * 4,
        out_specs=(VMEM,) * 2,
        scratch_shapes=[pltpu.VMEM((inst * 5 * rad, width), jnp.float32)] * 3,
        compiler_params=pltpu.CompilerParams(vmem_limit_bytes=40 * 2**20),
        name="finish",
    )(shifts, table, whole, base, smoothed)


def solution(mesh):
    in_specs = (P(None, "axial", "radial", "pitch"), P(None, None, "axial", "radial", "pitch"), P())
    out_specs = (
        P(None, None, "axial", "radial", "pitch"),
        P(None, None, "axial", "radial", "pitch"),
    )
    return jax.shard_map(local, mesh=mesh, in_specs=in_specs, out_specs=out_specs, check_vma=False)
```

```python
import functools
import math

import jax
import jax.numpy as jnp
import numpy as np
from jax import lax
from jax.experimental import pallas as pl
from jax.experimental.pallas import tpu as pltpu
from jax.sharding import PartitionSpec as P

COEFFS = (0.75, -0.15, 1.0 / 60.0)
GAMMA_LESS = 0.4
HIGHEST = lax.Precision.HIGHEST
MESH = pl.DeviceIdType.MESH
VMEM = pl.BlockSpec(memory_space=pltpu.VMEM)
HBM = pl.BlockSpec(memory_space=pltpu.HBM)


def filter_constants(extent):
    eps = float(extent * extent // 16)
    decay = 2.0 * eps / (1.0 + 2.0 * eps + math.sqrt(1.0 + 4.0 * eps))
    gain = 1.0 / (math.sqrt(1.0 + 4.0 * eps) * (1.0 - decay**extent))
    return decay, gain


def tables(width, extent):
    decay, gain = filter_constants(extent)
    points = np.arange(width)
    apart = np.abs(points[:, None] - points[None, :])
    green = gain * (decay**apart + decay ** (extent - apart))
    deriv = np.zeros((width, width))
    rims = np.zeros((8, width))
    picks = np.zeros((8, width))
    for offset, weight in enumerate(COEFFS):
        reach = offset + 1
        for i in range(width):
            if i + reach < width:
                deriv[i + reach, i] += weight
            else:
                rims[i + reach - width, i] += weight
            if i - reach >= 0:
                deriv[i - reach, i] -= weight
            else:
                rims[4 + i - reach + 3, i] -= weight
    for h in range(3):
        picks[h, h] = 1.0
        picks[4 + h, width - 3 + h] = 1.0
    sums = np.zeros((8, width))
    sums[0] = decay ** (width - 1.0 - points)
    sums[1] = decay ** (points + 0.0)
    spread = np.zeros((8, width))
    spread[0] = gain * decay ** (points + 1.0)
    spread[1] = gain * decay ** (width - points + 0.0)
    return np.concatenate([deriv, green, rims, picks, sums, spread]).astype(np.float32)


def dot(a, b):
    return jnp.dot(a, b, precision=HIGHEST, preferred_element_type=jnp.float32)


def dot_nt(a, b):
    return lax.dot_general(
        a, b, (((1,), (1,)), ((), ())), precision=HIGHEST, preferred_element_type=jnp.float32
    )


def dot_tn(a, b):
    return lax.dot_general(
        a, b, (((0,), (0,)), ((), ())), precision=HIGHEST, preferred_element_type=jnp.float32
    )


def exchange_kernel(
    count_p,
    count_r,
    shifts_hbm,
    density_hbm,
    moments_hbm,
    table_hbm,
    base,
    smoothed,
    landed,
    shifts,
    density,
    moments,
    table,
    plane_out,
    loop_in,
    lined_up,
    along_p,
    along_r,
    rim_out,
    rim_in,
    sum_out,
    sum_in,
    load_sem,
    cross_send,
    cross_recv,
    back_send,
    back_recv,
    rim_send,
    rim_recv,
    radial_send,
    radial_recv,
    sum_send,
    sum_recv,
):
    inst, planes, rad, width = density.shape
    rows = inst * 5 * planes * rad
    units = loop_in.shape[1]
    extent = width * count_p
    decay, _ = filter_constants(extent)
    p = lax.axis_index("pitch")
    r = lax.axis_index("radial")
    a = lax.axis_index("axial")
    plane = (planes - 1) * (1 - a)

    loads = [
        pltpu.make_async_copy(src, dst, load_sem.at[i])
        for i, (src, dst) in enumerate(
            (
                (density_hbm, density),
                (moments_hbm, moments),
                (table_hbm, table),
                (shifts_hbm, shifts),
            )
        )
    ]
    for load in loads:
        load.start()

    barrier = pltpu.get_barrier_semaphore()
    for k in range(count_p):
        where = lax.rem(p + k, count_p)
        if k > 0:
            pl.semaphore_signal(barrier, inc=1, device_id=(where, r, a), device_id_type=MESH)
        pl.semaphore_signal(barrier, inc=1, device_id=(where, r, 1 - a), device_id_type=MESH)
    for k in (1, count_r - 1):
        pl.semaphore_signal(
            barrier, inc=1, device_id=(p, lax.rem(r + k, count_r), a), device_id_type=MESH
        )

    loads[0].wait()
    loads[1].wait()
    for n in range(inst):
        plane_out[5 * n] = density[n, plane]
        for v in range(4):
            plane_out[5 * n + 1 + v] = moments[n, v, plane]
    if count_p * units > 5 * inst:
        spare = count_p * units - 5 * inst
        plane_out[5 * inst :] = jnp.zeros((spare, rad, width), jnp.float32)

    pl.semaphore_wait(barrier, 2 * count_p + 1)

    def cross(k):
        where = lax.rem(p + k, count_p)
        return pltpu.make_async_remote_copy(
            src_ref=plane_out.at[pl.ds(where * units, units)],
            dst_ref=loop_in.at[p],
            send_sem=cross_send.at[k],
            recv_sem=cross_recv.at[k],
            device_id=(where, r, 1 - a),
            device_id_type=MESH,
        )

    def crossed(k):
        source = lax.rem(p + count_p - k, count_p)
        return pltpu.make_async_remote_copy(
            src_ref=plane_out.at[0:units],
            dst_ref=loop_in.at[source],
            send_sem=cross_send.at[k],
            recv_sem=cross_recv.at[k],
            device_id=(source, r, 1 - a),
            device_id_type=MESH,
        )

    order = sorted(range(count_p), key=lambda k: -min(k, count_p - k))
    for k in order:
        cross(k).start()

    rho = density[...]
    axial_m, radial_m, pitch_m, energy = (moments[:, v] for v in range(4))
    inverse = 1.0 / rho
    pressure = GAMMA_LESS * (
        energy - 0.5 * (axial_m * axial_m + radial_m * radial_m + pitch_m * pitch_m) * inverse
    )
    pitch_v = pitch_m * inverse
    radial_v = radial_m * inverse
    enthalpy = energy + pressure
    along_p[:, 0] = pitch_m
    along_p[:, 1] = axial_m * pitch_v
    along_p[:, 2] = radial_m * pitch_v
    along_p[:, 3] = pitch_m * pitch_v + pressure
    along_p[:, 4] = enthalpy * pitch_v
    mine = slice(rad, 2 * rad)
    along_r[:, 0, :, mine] = radial_m
    along_r[:, 1, :, mine] = axial_m * radial_v
    along_r[:, 2, :, mine] = radial_m * radial_v + pressure
    along_r[:, 3, :, mine] = pitch_m * radial_v
    along_r[:, 4, :, mine] = enthalpy * radial_v

    @pl.when(r == 0)
    def _():
        along_r[:, :, :, 0:rad] = jnp.zeros((inst, 5, planes, rad, width), jnp.float32)

    @pl.when(r == count_r - 1)
    def _():
        along_r[:, :, :, 2 * rad : 3 * rad] = jnp.zeros(
            (inst, 5, planes, rad, width), jnp.float32
        )

    def radial_copy(up):
        if up:
            src = along_r.at[:, :, :, 2 * rad - 3 : 2 * rad]
            dst = along_r.at[:, :, :, rad - 3 : rad]
            target = r + 1
        else:
            src = along_r.at[:, :, :, rad : rad + 3]
            dst = along_r.at[:, :, :, 2 * rad : 2 * rad + 3]
            target = r - 1
        return pltpu.make_async_remote_copy(
            src_ref=src,
            dst_ref=dst,
            send_sem=radial_send.at[int(up)],
            recv_sem=radial_recv.at[int(up)],
            device_id=(p, target, a),
            device_id_type=MESH,
        )

    pl.when(r < count_r - 1)(lambda: radial_copy(True).start())
    pl.when(r > 0)(lambda: radial_copy(False).start())

    loads[2].wait()
    loads[3].wait()
    flat_p = along_p[...].reshape(rows, width)
    rim_out[...] = dot_nt(table[2 * width + 8 : 2 * width + 16], flat_p)

    def rim_copy(up):
        part = slice(4, 8) if up else slice(0, 4)
        return pltpu.make_async_remote_copy(
            src_ref=rim_out.at[part],
            dst_ref=rim_in.at[part],
            send_sem=rim_send.at[int(up)],
            recv_sem=rim_recv.at[int(up)],
            device_id=(lax.rem(p + (1 if up else count_p - 1), count_p), r, a),
            device_id_type=MESH,
        )

    rim_copy(True).start()
    rim_copy(False).start()

    base[...] = dot(flat_p, table[0:width]).reshape(inst, 5, planes, rad, width)
    for v, field in enumerate((rho, axial_m, radial_m, pitch_m, energy)):
        total = None
        for k in range(1, (inst + 1) // 2):
            weight = 0.5 * (-1.0) ** k / math.sin(math.pi * k / inst)
            back = jnp.concatenate([field[inst - k :], field[: inst - k]], axis=0)
            ahead = jnp.concatenate([field[k:], field[:k]], axis=0)
            term = weight * (back - ahead)
            total = term if total is None else total + term
        for b in range(planes):
            on = jnp.where(plane == b, 1.0, 0.0).astype(jnp.float32)
            base[:, v, b] += total[:, b] - on * field[:, b]

    for k in order[::-1]:
        crossed(k).wait_recv()
    lane = lax.broadcasted_iota(jnp.int32, (rad, width), 1)
    for u in range(units):
        n = lax.min(lax.div(p * units + u, 5), inst - 1)
        shift = shifts[n]
        start = lax.rem(jnp.where(a == 1, extent - shift, shift), extent)
        block = lax.div(start, width)
        inside = start - block * width
        turn = lax.rem(width - inside, width)
        parts = [loop_in[lax.rem(block + b, count_p), u] for b in range(count_p)]
        for b in range(count_p):
            merged = jnp.where(lane >= inside, parts[b], parts[(b + 1) % count_p])
            lined_up[b, u] = pltpu.roll(merged, turn, 1)
    held = units * rad
    sums = [
        dot_nt(
            table[2 * width + 16 : 2 * width + 24],
            lined_up[b, 0:units].reshape(held, width),
        )
        for b in range(count_p)
    ]
    for b in range(count_p):
        ahead = None
        behind = None
        for k in range(1, count_p):
            other = sums[(b - k) % count_p]
            left = decay ** (width * (k - 1.0)) * other[0:1]
            right = decay ** (width * (count_p - k - 1.0)) * other[1:2]
            ahead = left if ahead is None else ahead + left
            behind = right if behind is None else behind + right
        carried = jnp.concatenate([ahead, behind, jnp.zeros((6, held), jnp.float32)], axis=0)
        if held < width:
            carried = jnp.concatenate(
                [carried, jnp.zeros((8, width - held), jnp.float32)], axis=1
            )
        lined_up[b, units] = carried

    def back(k):
        where = lax.rem(p + k, count_p)
        return pltpu.make_async_remote_copy(
            src_ref=lined_up.at[where],
            dst_ref=landed.at[p],
            send_sem=back_send.at[k - 1],
            recv_sem=back_recv.at[k - 1],
            device_id=(where, r, a),
            device_id_type=MESH,
        )

    def landing(k):
        source = lax.rem(p + count_p - k, count_p)
        return pltpu.make_async_remote_copy(
            src_ref=lined_up.at[source],
            dst_ref=landed.at[source],
            send_sem=back_send.at[k - 1],
            recv_sem=back_recv.at[k - 1],
            device_id=(source, r, a),
            device_id_type=MESH,
        )

    for k in order:
        if k > 0:
            back(k).start()
    landed[p] = lined_up[p]

    pl.when(r > 0)(lambda: radial_copy(True).wait_recv())
    pl.when(r < count_r - 1)(lambda: radial_copy(False).wait_recv())
    rim_copy(True).wait_recv()
    rim_copy(False).wait_recv()
    across = dot_tn(rim_in[...], table[2 * width : 2 * width + 8])
    radial = None
    for offset, weight in enumerate(COEFFS):
        k = offset + 1
        term = weight * (
            along_r[:, :, :, rad + k : 2 * rad + k] - along_r[:, :, :, rad - k : 2 * rad - k]
        )
        radial = term if radial is None else radial + term
    base[...] += across.reshape(inst, 5, planes, rad, width) + radial
    flat = base[...].reshape(rows, width)
    sum_out[...] = dot_nt(table[2 * width + 16 : 2 * width + 24], flat)

    def sum_copy(k):
        return pltpu.make_async_remote_copy(
            src_ref=sum_out.at[0:2],
            dst_ref=sum_in.at[k - 1],
            send_sem=sum_send.at[k - 1],
            recv_sem=sum_recv.at[k - 1],
            device_id=(lax.rem(p + k, count_p), r, a),
            device_id_type=MESH,
        )

    for k in range(1, count_p):
        sum_copy(k).start()
    smoothed[...] = dot(flat, table[width : 2 * width]).reshape(inst, 5, planes, rad, width)
    ahead = None
    behind = None
    for k in range(1, count_p):
        sum_copy(k).wait_recv()
        left = decay ** (width * (k - 1.0)) * sum_in[k - 1, 0:1]
        right = decay ** (width * (count_p - k - 1.0)) * sum_in[k - 1, 1:2]
        ahead = left if ahead is None else ahead + left
        behind = right if behind is None else behind + right
    carried = jnp.concatenate([ahead, behind, jnp.zeros((6, rows), jnp.float32)], axis=0)
    smoothed[...] += dot_tn(carried, table[2 * width + 24 : 2 * width + 32]).reshape(
        inst, 5, planes, rad, width
    )

    for k in range(1, count_p):
        landing(k).wait_recv()
        back(k).wait_send()
        sum_copy(k).wait_send()
    for k in range(count_p):
        cross(k).wait_send()
    pl.when(r < count_r - 1)(lambda: radial_copy(True).wait_send())
    pl.when(r > 0)(lambda: radial_copy(False).wait_send())
    rim_copy(True).wait_send()
    rim_copy(False).wait_send()


def finish_kernel(count_p, table, landed, base, smoothed, residual, update):
    inst, _, planes, rad, width = base.shape
    units = landed.shape[1] - 1
    held = units * rad
    a = lax.axis_index("axial")
    plane = (planes - 1) * (1 - a)
    spread = table[2 * width + 24 : 2 * width + 32]
    residual[...] = base[...]
    update[...] = smoothed[...]
    for i in range(count_p):
        share = landed[i, 0:units].reshape(held, width)
        filtered = dot(share, table[width : 2 * width]) + dot_tn(landed[i, units], spread)[:held]
        for u in range(units):
            unit = i * units + u
            if unit < 5 * inst:
                n, v = divmod(unit, 5)
                residual[n, v, plane] += share[u * rad : (u + 1) * rad]
                update[n, v, plane] += filtered[u * rad : (u + 1) * rad]


def local(density, moments, shifts):
    count_p = lax.axis_size("pitch")
    count_r = lax.axis_size("radial")
    inst, planes, rad, width = density.shape
    rows = inst * 5 * planes * rad
    units = -(-5 * inst // count_p)
    table = jnp.asarray(tables(width, width * count_p))
    block = jax.ShapeDtypeStruct((inst, 5, planes, rad, width), jnp.float32)
    dma = pltpu.SemaphoreType.DMA
    base, smoothed, landed = pl.pallas_call(
        functools.partial(exchange_kernel, count_p, count_r),
        out_shape=(
            block,
            block,
            jax.ShapeDtypeStruct((count_p, units + 1, rad, width), jnp.float32),
        ),
        in_specs=[HBM] * 4,
        out_specs=(VMEM,) * 3,
        scratch_shapes=[
            pltpu.SMEM((inst,), jnp.int32),
            pltpu.VMEM(density.shape, jnp.float32),
            pltpu.VMEM(moments.shape, jnp.float32),
            pltpu.VMEM(table.shape, jnp.float32),
            pltpu.VMEM((count_p * units, rad, width), jnp.float32),
            pltpu.VMEM((count_p, units, rad, width), jnp.float32),
            pltpu.VMEM((count_p, units + 1, rad, width), jnp.float32),
            pltpu.VMEM((inst, 5, planes, rad, width), jnp.float32),
            pltpu.VMEM((inst, 5, planes, 3 * rad, width), jnp.float32),
            pltpu.VMEM((8, rows), jnp.float32),
            pltpu.VMEM((8, rows), jnp.float32),
            pltpu.VMEM((8, rows), jnp.float32),
            pltpu.VMEM((count_p - 1, 2, rows), jnp.float32),
            dma((4,)),
            dma((count_p,)),
            dma((count_p,)),
            dma((count_p - 1,)),
            dma((count_p - 1,)),
            dma((2,)),
            dma((2,)),
            dma((2,)),
            dma((2,)),
            dma((count_p - 1,)),
            dma((count_p - 1,)),
        ],
        compiler_params=pltpu.CompilerParams(
            collective_id=0, has_side_effects=True, vmem_limit_bytes=40 * 2**20
        ),
        name="exchange",
    )(shifts, density, moments, table)
    return pl.pallas_call(
        functools.partial(finish_kernel, count_p),
        out_shape=(block, block),
        in_specs=[VMEM] * 4,
        out_specs=(VMEM,) * 2,
        compiler_params=pltpu.CompilerParams(vmem_limit_bytes=40 * 2**20),
        name="finish",
    )(table, landed, base, smoothed)


def solution(mesh):
    in_specs = (P(None, "axial", "radial", "pitch"), P(None, None, "axial", "radial", "pitch"), P())
    out_specs = (
        P(None, None, "axial", "radial", "pitch"),
        P(None, None, "axial", "radial", "pitch"),
    )
    return jax.shard_map(local, mesh=mesh, in_specs=in_specs, out_specs=out_specs, check_vma=False)
```

```python
import functools
import math

import jax
import jax.numpy as jnp
import numpy as np
from jax import lax
from jax.experimental import pallas as pl
from jax.experimental.pallas import tpu as pltpu
from jax.sharding import PartitionSpec as P

COEFFS = (0.75, -0.15, 1.0 / 60.0)
GAMMA_LESS = 0.4
HIGHEST = lax.Precision.HIGHEST
MESH = pl.DeviceIdType.MESH
VMEM_LIMIT = 60 * 2**20
HBM = pl.BlockSpec(memory_space=pltpu.HBM)


def filter_constants(extent):
    eps = float(extent * extent // 16)
    decay = 2.0 * eps / (1.0 + 2.0 * eps + math.sqrt(1.0 + 4.0 * eps))
    gain = 1.0 / (math.sqrt(1.0 + 4.0 * eps) * (1.0 - decay**extent))
    return decay, gain


def tables(width, extent):
    decay, gain = filter_constants(extent)
    points = np.arange(width)
    apart = np.abs(points[:, None] - points[None, :])
    green = gain * (decay**apart + decay ** (extent - apart))
    deriv = np.zeros((width, width))
    rims = np.zeros((8, width))
    picks = np.zeros((8, width))
    for offset, weight in enumerate(COEFFS):
        reach = offset + 1
        for i in range(width):
            if i + reach < width:
                deriv[i + reach, i] += weight
            else:
                rims[i + reach - width, i] += weight
            if i - reach >= 0:
                deriv[i - reach, i] -= weight
            else:
                rims[4 + i - reach + 3, i] -= weight
    for h in range(3):
        picks[h, h] = 1.0
        picks[4 + h, width - 3 + h] = 1.0
    sums = np.zeros((8, width))
    sums[0] = decay ** (width - 1.0 - points)
    sums[1] = decay ** (points + 0.0)
    spread = np.zeros((8, width))
    spread[0] = gain * decay ** (points + 1.0)
    spread[1] = gain * decay ** (width - points + 0.0)
    return np.concatenate([deriv, green, rims, picks, sums, spread]).astype(np.float32)


def dot(a, b):
    return jnp.dot(a, b, precision=HIGHEST, preferred_element_type=jnp.float32)


def dot_nt(a, b):
    return lax.dot_general(
        a, b, (((1,), (1,)), ((), ())), precision=HIGHEST, preferred_element_type=jnp.float32
    )


def dot_tn(a, b):
    return lax.dot_general(
        a, b, (((0,), (0,)), ((), ())), precision=HIGHEST, preferred_element_type=jnp.float32
    )


def exchange_kernel(
    count_p,
    count_r,
    shifts_hbm,
    density_hbm,
    moments_hbm,
    table_hbm,
    base_hbm,
    smoothed_hbm,
    landed,
    base,
    smoothed,
    shifts,
    density,
    moments,
    table,
    plane_out,
    loop_in,
    lined_up,
    along_p,
    along_r,
    rim_out,
    rim_in,
    sum_out,
    sum_in,
    load_sem,
    store_sem,
    cross_send,
    cross_recv,
    back_send,
    back_recv,
    rim_send,
    rim_recv,
    radial_send,
    radial_recv,
    sum_send,
    sum_recv,
):
    inst, planes, rad, width = density.shape
    rows = inst * 5 * planes * rad
    units = loop_in.shape[1]
    extent = width * count_p
    decay, _ = filter_constants(extent)
    p = lax.axis_index("pitch")
    r = lax.axis_index("radial")
    a = lax.axis_index("axial")
    plane = (planes - 1) * (1 - a)

    loads = [
        pltpu.make_async_copy(src, dst, load_sem.at[i])
        for i, (src, dst) in enumerate(
            (
                (density_hbm, density),
                (moments_hbm, moments),
                (table_hbm, table),
                (shifts_hbm, shifts),
            )
        )
    ]
    for load in loads:
        load.start()

    barrier = pltpu.get_barrier_semaphore()
    for k in range(count_p):
        where = lax.rem(p + k, count_p)
        if k > 0:
            pl.semaphore_signal(barrier, inc=1, device_id=(where, r, a), device_id_type=MESH)
        pl.semaphore_signal(barrier, inc=1, device_id=(where, r, 1 - a), device_id_type=MESH)
    for k in (1, count_r - 1):
        pl.semaphore_signal(
            barrier, inc=1, device_id=(p, lax.rem(r + k, count_r), a), device_id_type=MESH
        )

    loads[0].wait()
    loads[1].wait()
    for n in range(inst):
        plane_out[5 * n] = density[n, plane]
        for v in range(4):
            plane_out[5 * n + 1 + v] = moments[n, v, plane]
    if count_p * units > 5 * inst:
        spare = count_p * units - 5 * inst
        plane_out[5 * inst :] = jnp.zeros((spare, rad, width), jnp.float32)

    pl.semaphore_wait(barrier, 2 * count_p + 1)

    def cross(k):
        where = lax.rem(p + k, count_p)
        return pltpu.make_async_remote_copy(
            src_ref=plane_out.at[pl.ds(where * units, units)],
            dst_ref=loop_in.at[p],
            send_sem=cross_send.at[k],
            recv_sem=cross_recv.at[k],
            device_id=(where, r, 1 - a),
            device_id_type=MESH,
        )

    def crossed(k):
        source = lax.rem(p + count_p - k, count_p)
        return pltpu.make_async_remote_copy(
            src_ref=plane_out.at[0:units],
            dst_ref=loop_in.at[source],
            send_sem=cross_send.at[k],
            recv_sem=cross_recv.at[k],
            device_id=(source, r, 1 - a),
            device_id_type=MESH,
        )

    order = sorted(range(count_p), key=lambda k: -min(k, count_p - k))
    for k in order:
        cross(k).start()

    rho = density[...]
    axial_m, radial_m, pitch_m, energy = (moments[:, v] for v in range(4))
    inverse = 1.0 / rho
    pressure = GAMMA_LESS * (
        energy - 0.5 * (axial_m * axial_m + radial_m * radial_m + pitch_m * pitch_m) * inverse
    )
    pitch_v = pitch_m * inverse
    radial_v = radial_m * inverse
    enthalpy = energy + pressure
    along_p[:, 0] = pitch_m
    along_p[:, 1] = axial_m * pitch_v
    along_p[:, 2] = radial_m * pitch_v
    along_p[:, 3] = pitch_m * pitch_v + pressure
    along_p[:, 4] = enthalpy * pitch_v
    mine = slice(rad, 2 * rad)
    along_r[:, 0, :, mine] = radial_m
    along_r[:, 1, :, mine] = axial_m * radial_v
    along_r[:, 2, :, mine] = radial_m * radial_v + pressure
    along_r[:, 3, :, mine] = pitch_m * radial_v
    along_r[:, 4, :, mine] = enthalpy * radial_v

    @pl.when(r == 0)
    def _():
        along_r[:, :, :, 0:rad] = jnp.zeros((inst, 5, planes, rad, width), jnp.float32)

    @pl.when(r == count_r - 1)
    def _():
        along_r[:, :, :, 2 * rad : 3 * rad] = jnp.zeros(
            (inst, 5, planes, rad, width), jnp.float32
        )

    def radial_copy(up):
        if up:
            src = along_r.at[:, :, :, 2 * rad - 3 : 2 * rad]
            dst = along_r.at[:, :, :, rad - 3 : rad]
            target = r + 1
        else:
            src = along_r.at[:, :, :, rad : rad + 3]
            dst = along_r.at[:, :, :, 2 * rad : 2 * rad + 3]
            target = r - 1
        return pltpu.make_async_remote_copy(
            src_ref=src,
            dst_ref=dst,
            send_sem=radial_send.at[int(up)],
            recv_sem=radial_recv.at[int(up)],
            device_id=(p, target, a),
            device_id_type=MESH,
        )

    pl.when(r < count_r - 1)(lambda: radial_copy(True).start())
    pl.when(r > 0)(lambda: radial_copy(False).start())

    loads[2].wait()
    loads[3].wait()
    flat_p = along_p[...].reshape(rows, width)
    rim_out[...] = dot_nt(table[2 * width + 8 : 2 * width + 16], flat_p)

    def rim_copy(up):
        part = slice(4, 8) if up else slice(0, 4)
        return pltpu.make_async_remote_copy(
            src_ref=rim_out.at[part],
            dst_ref=rim_in.at[part],
            send_sem=rim_send.at[int(up)],
            recv_sem=rim_recv.at[int(up)],
            device_id=(lax.rem(p + (1 if up else count_p - 1), count_p), r, a),
            device_id_type=MESH,
        )

    rim_copy(True).start()
    rim_copy(False).start()

    base[...] = dot(flat_p, table[0:width]).reshape(inst, 5, planes, rad, width)
    for v, field in enumerate((rho, axial_m, radial_m, pitch_m, energy)):
        total = None
        for k in range(1, (inst + 1) // 2):
            weight = 0.5 * (-1.0) ** k / math.sin(math.pi * k / inst)
            back = jnp.concatenate([field[inst - k :], field[: inst - k]], axis=0)
            ahead = jnp.concatenate([field[k:], field[:k]], axis=0)
            term = weight * (back - ahead)
            total = term if total is None else total + term
        for b in range(planes):
            on = jnp.where(plane == b, 1.0, 0.0).astype(jnp.float32)
            base[:, v, b] += total[:, b] - on * field[:, b]

    pl.when(r > 0)(lambda: radial_copy(True).wait_recv())
    pl.when(r < count_r - 1)(lambda: radial_copy(False).wait_recv())
    rim_copy(True).wait_recv()
    rim_copy(False).wait_recv()
    across = dot_tn(rim_in[...], table[2 * width : 2 * width + 8])
    radial = None
    for offset, weight in enumerate(COEFFS):
        k = offset + 1
        term = weight * (
            along_r[:, :, :, rad + k : 2 * rad + k] - along_r[:, :, :, rad - k : 2 * rad - k]
        )
        radial = term if radial is None else radial + term
    base[...] += across.reshape(inst, 5, planes, rad, width) + radial
    flat = base[...].reshape(rows, width)
    sum_out[...] = dot_nt(table[2 * width + 16 : 2 * width + 24], flat)

    def sum_copy(k):
        return pltpu.make_async_remote_copy(
            src_ref=sum_out.at[0:2],
            dst_ref=sum_in.at[k - 1],
            send_sem=sum_send.at[k - 1],
            recv_sem=sum_recv.at[k - 1],
            device_id=(lax.rem(p + k, count_p), r, a),
            device_id_type=MESH,
        )

    for k in range(1, count_p):
        sum_copy(k).start()
    store_base = pltpu.make_async_copy(base, base_hbm, store_sem.at[0])
    store_base.start()
    smoothed[...] = dot(flat, table[width : 2 * width]).reshape(inst, 5, planes, rad, width)

    for k in order[::-1]:
        crossed(k).wait_recv()
    lane = lax.broadcasted_iota(jnp.int32, (rad, width), 1)
    for u in range(units):
        n = lax.min(lax.div(p * units + u, 5), inst - 1)
        shift = shifts[n]
        start = lax.rem(jnp.where(a == 1, extent - shift, shift), extent)
        block = lax.div(start, width)
        inside = start - block * width
        turn = lax.rem(width - inside, width)
        parts = [loop_in[lax.rem(block + b, count_p), u] for b in range(count_p)]
        for b in range(count_p):
            merged = jnp.where(lane >= inside, parts[b], parts[(b + 1) % count_p])
            lined_up[b, u] = pltpu.roll(merged, turn, 1)
    held = units * rad
    sums = [
        dot_nt(
            table[2 * width + 16 : 2 * width + 24],
            lined_up[b, 0:units].reshape(held, width),
        )
        for b in range(count_p)
    ]
    for b in range(count_p):
        ahead = None
        behind = None
        for k in range(1, count_p):
            other = sums[(b - k) % count_p]
            left = decay ** (width * (k - 1.0)) * other[0:1]
            right = decay ** (width * (count_p - k - 1.0)) * other[1:2]
            ahead = left if ahead is None else ahead + left
            behind = right if behind is None else behind + right
        carried = jnp.concatenate([ahead, behind, jnp.zeros((6, held), jnp.float32)], axis=0)
        if held < width:
            carried = jnp.concatenate(
                [carried, jnp.zeros((8, width - held), jnp.float32)], axis=1
            )
        lined_up[b, units] = carried

    def back(k):
        where = lax.rem(p + k, count_p)
        return pltpu.make_async_remote_copy(
            src_ref=lined_up.at[where],
            dst_ref=landed.at[p],
            send_sem=back_send.at[k - 1],
            recv_sem=back_recv.at[k - 1],
            device_id=(where, r, a),
            device_id_type=MESH,
        )

    def landing(k):
        source = lax.rem(p + count_p - k, count_p)
        return pltpu.make_async_remote_copy(
            src_ref=lined_up.at[source],
            dst_ref=landed.at[source],
            send_sem=back_send.at[k - 1],
            recv_sem=back_recv.at[k - 1],
            device_id=(source, r, a),
            device_id_type=MESH,
        )

    for k in order:
        if k > 0:
            back(k).start()
    keep = pltpu.make_async_copy(lined_up.at[p], landed.at[p], store_sem.at[2])
    keep.start()

    ahead = None
    behind = None
    for k in range(1, count_p):
        sum_copy(k).wait_recv()
        left = decay ** (width * (k - 1.0)) * sum_in[k - 1, 0:1]
        right = decay ** (width * (count_p - k - 1.0)) * sum_in[k - 1, 1:2]
        ahead = left if ahead is None else ahead + left
        behind = right if behind is None else behind + right
    carried = jnp.concatenate([ahead, behind, jnp.zeros((6, rows), jnp.float32)], axis=0)
    smoothed[...] += dot_tn(carried, table[2 * width + 24 : 2 * width + 32]).reshape(
        inst, 5, planes, rad, width
    )

    store_smoothed = pltpu.make_async_copy(smoothed, smoothed_hbm, store_sem.at[1])
    store_smoothed.start()

    store_base.wait()
    keep.wait()
    store_smoothed.wait()
    for k in range(1, count_p):
        landing(k).wait_recv()
        back(k).wait_send()
        sum_copy(k).wait_send()
    for k in range(count_p):
        cross(k).wait_send()
    pl.when(r < count_r - 1)(lambda: radial_copy(True).wait_send())
    pl.when(r > 0)(lambda: radial_copy(False).wait_send())
    rim_copy(True).wait_send()
    rim_copy(False).wait_send()


def finish_kernel(
    count_p,
    table_hbm,
    landed_hbm,
    base_hbm,
    smoothed_hbm,
    residual_hbm,
    update_hbm,
    table,
    landed,
    residual,
    update,
    load_sem,
    store_sem,
):
    loads = [
        pltpu.make_async_copy(src, dst, load_sem.at[i])
        for i, (src, dst) in enumerate(
            (
                (table_hbm, table),
                (landed_hbm, landed),
                (smoothed_hbm, update),
                (base_hbm, residual),
            )
        )
    ]
    for load in loads:
        load.start()
    inst, _, planes, rad, width = residual.shape
    units = landed.shape[1] - 1
    held = units * rad
    a = lax.axis_index("axial")
    plane = (planes - 1) * (1 - a)
    for load in loads:
        load.wait()
    spread = table[2 * width + 24 : 2 * width + 32]
    for i in range(count_p):
        share = landed[i, 0:units].reshape(held, width)
        filtered = dot(share, table[width : 2 * width]) + dot_tn(landed[i, units], spread)[:held]
        for u in range(units):
            unit = i * units + u
            if unit < 5 * inst:
                n, v = divmod(unit, 5)
                residual[n, v, plane] += share[u * rad : (u + 1) * rad]
                update[n, v, plane] += filtered[u * rad : (u + 1) * rad]
    stores = [
        pltpu.make_async_copy(residual, residual_hbm, store_sem.at[0]),
        pltpu.make_async_copy(update, update_hbm, store_sem.at[1]),
    ]
    for store in stores:
        store.start()
    for store in stores:
        store.wait()


def local(density, moments, shifts):
    count_p = lax.axis_size("pitch")
    count_r = lax.axis_size("radial")
    inst, planes, rad, width = density.shape
    rows = inst * 5 * planes * rad
    units = -(-5 * inst // count_p)
    table = jnp.asarray(tables(width, width * count_p))
    block = jax.ShapeDtypeStruct((inst, 5, planes, rad, width), jnp.float32)
    dma = pltpu.SemaphoreType.DMA
    base, smoothed, landed = pl.pallas_call(
        functools.partial(exchange_kernel, count_p, count_r),
        out_shape=(
            block,
            block,
            jax.ShapeDtypeStruct((count_p, units + 1, rad, width), jnp.float32),
        ),
        in_specs=[HBM] * 4,
        out_specs=(HBM,) * 3,
        scratch_shapes=[
            pltpu.VMEM(block.shape, jnp.float32),
            pltpu.VMEM(block.shape, jnp.float32),
            pltpu.SMEM((inst,), jnp.int32),
            pltpu.VMEM(density.shape, jnp.float32),
            pltpu.VMEM(moments.shape, jnp.float32),
            pltpu.VMEM(table.shape, jnp.float32),
            pltpu.VMEM((count_p * units, rad, width), jnp.float32),
            pltpu.VMEM((count_p, units, rad, width), jnp.float32),
            pltpu.VMEM((count_p, units + 1, rad, width), jnp.float32),
            pltpu.VMEM((inst, 5, planes, rad, width), jnp.float32),
            pltpu.VMEM((inst, 5, planes, 3 * rad, width), jnp.float32),
            pltpu.VMEM((8, rows), jnp.float32),
            pltpu.VMEM((8, rows), jnp.float32),
            pltpu.VMEM((8, rows), jnp.float32),
            pltpu.VMEM((count_p - 1, 2, rows), jnp.float32),
            dma((4,)),
            dma((3,)),
            dma((count_p,)),
            dma((count_p,)),
            dma((count_p - 1,)),
            dma((count_p - 1,)),
            dma((2,)),
            dma((2,)),
            dma((2,)),
            dma((2,)),
            dma((count_p - 1,)),
            dma((count_p - 1,)),
        ],
        compiler_params=pltpu.CompilerParams(
            collective_id=0, has_side_effects=True, vmem_limit_bytes=VMEM_LIMIT
        ),
        name="exchange",
    )(shifts, density, moments, table)
    return pl.pallas_call(
        functools.partial(finish_kernel, count_p),
        out_shape=(block, block),
        in_specs=[HBM] * 4,
        out_specs=(HBM,) * 2,
        scratch_shapes=[
            pltpu.VMEM(table.shape, jnp.float32),
            pltpu.VMEM((count_p, units + 1, rad, width), jnp.float32),
            pltpu.VMEM(block.shape, jnp.float32),
            pltpu.VMEM(block.shape, jnp.float32),
            dma((4,)),
            dma((2,)),
        ],
        compiler_params=pltpu.CompilerParams(vmem_limit_bytes=VMEM_LIMIT),
        name="finish",
    )(table, landed, base, smoothed)


def solution(mesh):
    in_specs = (P(None, "axial", "radial", "pitch"), P(None, None, "axial", "radial", "pitch"), P())
    out_specs = (
        P(None, None, "axial", "radial", "pitch"),
        P(None, None, "axial", "radial", "pitch"),
    )
    return jax.shard_map(local, mesh=mesh, in_specs=in_specs, out_specs=out_specs, check_vma=False)
```
